512 devices in a mesh: code: 128 (over y, z, core), item: 4 (over x).
Axes of the slice: x: 4, y: 8, z: 8, core: 2. Of those that a mesh axis runs over, the one named last changes fastest.
Arguments:
- hidden: bfloat16 [65536, 1024], P(('code', 'item')), may hold values from -80 to 80
- norm_gain: bfloat16 [1024], replicated, may hold values from 0.099609375 to 1.8984375
- first_weight: bfloat16 [1024, 1024], P('item'), may hold values from -0.1875 to 0.1875
- second_weight: bfloat16 [1024, 1024], P('item'), may hold values from -0.1875 to 0.1875
- codes: int32 [65536, 3], P(('code', 'item')), may hold values from 0 to 8191, as said below
- codebook: float32 [3, 8192, 1024], P(None, 'code'), may hold values from -3 to 3
- embed_avg: float32 [3, 8192, 1024], P(None, 'code'), may hold values from -24 to 24
- cluster_size: float32 [3, 8192], P(None, 'code'), may hold values from 4 to 64
Outputs:
- residual: bfloat16 [65536, 1024], P(('code', 'item'))
- cluster_new: float32 [3, 8192], P(None, 'code')
- avg_new: float32 [3, 8192, 1024], P(None, 'code')
- codebook_new: float32 [3, 8192, 1024], P(None, 'code')
The draws below stay inside these ranges and needn't reach their ends.
Inputs may be any that keep to these rules, and one draw needn't show every extreme that they name: `codes`: among the items of one device (aligned blocks of 128 rows), at most 2 have, at one level, a code whose value divided by 64 is the same; at every level of every block some such quotient is shared by exactly 2 items.
All inputs are finite; a program needn't handle non-finite values.
Results may differ from the reference program's by a relative error of at most 0.0053.
Values may be sent and summed in bfloat16 or wider, within the bound.
A program may use at most 64 MiB of HBM per device.

```python
import math
import jax
import jax.numpy as jnp
from jax import lax

D = 1024
CODE_DEV = 64
LEVELS = 3
ITEM_DEV = 128
CODES = 8192
ITEMS = 65536
CAP = 2


def draw_hidden(key, part):
    key = jax.random.fold_in(key, 5)
    first = jax.random.fold_in(key, 0)
    second = jax.random.fold_in(key, 1)
    fourth = jax.random.fold_in(key, 3)
    column_scale = jnp.exp(jax.random.uniform(fourth, (1, D), minval=0.0, maxval=2.3))
    base = jax.random.normal(first, (ITEMS, D))
    row_scale = jnp.exp(jax.random.uniform(second, (ITEMS, 1), minval=0.0, maxval=2.3))
    values = base * row_scale * column_scale * 0.3
    return jnp.clip(values, -80.0, 80.0).astype(jnp.bfloat16)


def draw_codes(key, part):
    key = jax.random.fold_in(key, 11)
    owners = CODES // CODE_DEV
    pool = owners * CAP
    blocks = ITEMS // ITEM_DEV

    def one_block(index):
        block_key = jax.random.fold_in(key, index)
        columns = []
        for level in range(LEVELS):
            level_key = jax.random.fold_in(block_key, level)
            key_full, key_rest, key_order, key_offset = jax.random.split(level_key, 4)
            full = jax.random.randint(key_full, (), 0, owners)
            rest = jax.random.permutation(key_rest, pool - CAP)[:ITEM_DEV - CAP]
            places = jnp.concatenate([jnp.arange(CAP, dtype=jnp.int32), rest.astype(jnp.int32) + CAP])
            owner = (places // CAP + full) % owners
            owner = jax.random.permutation(key_order, owner)
            offset = jax.random.randint(key_offset, (ITEM_DEV,), 0, CODE_DEV)
            columns.append(owner * CODE_DEV + offset)
        return jnp.stack(columns, axis=1)
    drawn = jax.lax.map(one_block, jnp.arange(blocks))
    return drawn.reshape(ITEMS, LEVELS).astype(jnp.int32)


def level_of(stream_key, dims, cuts, smallest, top_value):
    def one(position, shards_of):
        heights = jax.random.uniform(jax.random.fold_in(jax.random.fold_in(stream_key, 6), position), (shards_of,), jnp.float32, smallest / len(cuts), top_value / len(cuts))
        return jnp.repeat(jnp.exp(heights), dims[position] // shards_of).reshape((-1,) + (1,) * (len(dims) - position - 1))

    gain = one(*cuts[0])
    for cut in cuts[1:]:
        gain = gain * one(*cut)
    return gain


def centred(stream_key, dims, spread, most, cuts=(), kind=jnp.bfloat16):
    entries = spread * jax.random.normal(stream_key, dims, jnp.float32)
    if cuts:
        entries = entries * level_of(stream_key, dims, cuts, -0.22, 0.18)
    return jnp.clip(entries, -most, most).astype(kind)


def setup_inputs(seed: int = 0) -> dict:
    splits = jax.random.split(jax.random.key(seed), 9)
    hidden = draw_hidden(jax.random.fold_in(splits[8], 71), 0)
    norm_gain = jnp.clip(1.0 + 0.18 * jax.random.normal(splits[1], (D,), jnp.float32), 0.099609375, 1.8984375).astype(jnp.bfloat16)
    first_weight = centred(splits[2], (D, D), D ** -0.5, 0.1875, ((0, 4),))
    second_weight = centred(splits[3], (D, D), D ** -0.5, 0.1875, ((0, 4),))
    codes = draw_codes(jax.random.fold_in(splits[8], 71), 0)
    codebook = centred(splits[5], (LEVELS, CODES, D), 0.5, 3.0, ((1, 128),), jnp.float32)
    embed_avg = centred(splits[6], (LEVELS, CODES, D), 4.0, 24.0, ((1, 128),), jnp.float32)
    cluster_size = jnp.clip(jnp.exp(math.log(64.0) - 2.7725887 * jax.random.uniform(splits[7], (LEVELS, CODES), jnp.float32) ** level_of(splits[7], (LEVELS, CODES), ((1, 128),), -0.2, 0.2)), 4.0, 64.0)
    return {"hidden": hidden, "norm_gain": norm_gain, "first_weight": first_weight, "second_weight": second_weight, "codes": codes, "codebook": codebook, "embed_avg": embed_avg, "cluster_size": cluster_size}


ema_decay = 0.8
norm_eps = 1e-06

def reference(hidden, norm_gain, first_weight, second_weight, codes, codebook, embed_avg, cluster_size):
    values = hidden.astype(jnp.float32)
    power = lax.optimization_barrier(jnp.mean(values * values, axis=-1, keepdims=True))
    normed = (values * lax.rsqrt(power + norm_eps) * norm_gain.astype(jnp.float32)).astype(jnp.bfloat16)
    pre = jnp.dot(normed, first_weight, preferred_element_type=jnp.float32)
    middle = jax.nn.silu(pre).astype(jnp.bfloat16)
    resid = jnp.dot(middle, second_weight, preferred_element_type=jnp.float32)
    count_list = []
    sum_list = []
    for level in range(LEVELS):
        chosen = codes[:, level].astype(jnp.int32)
        sent = lax.optimization_barrier(resid.astype(jnp.bfloat16)).astype(jnp.float32)
        count_list.append(jax.ops.segment_sum(jnp.ones((ITEMS,), jnp.float32), chosen, num_segments=CODES))
        sum_list.append(jax.ops.segment_sum(sent, chosen, num_segments=CODES))
        quant = lax.optimization_barrier(jnp.take(codebook[level], chosen, axis=0).astype(jnp.bfloat16))
        resid = resid - quant.astype(jnp.float32)
    counts = jnp.stack(count_list)
    sums = jnp.stack(sum_list)
    cluster_new = ema_decay * cluster_size + (1.0 - ema_decay) * counts
    avg_new = ema_decay * embed_avg + (1.0 - ema_decay) * sums
    codebook_new = avg_new / cluster_new[:, :, None]
    return (resid.astype(jnp.bfloat16), cluster_new, avg_new, codebook_new)
```

```python
import functools

import jax
import jax.numpy as jnp
from jax import lax
from jax.experimental import pallas as pl
from jax.experimental.pallas import tpu as pltpu
from jax.sharding import PartitionSpec as P

ema_decay = 0.8
norm_eps = 1e-06
MESH = pl.DeviceIdType.MESH
LANES = 128
CHUNKS = 8
CORES = 2
F32, BF16, I32 = jnp.float32, jnp.bfloat16, jnp.int32


def grid_of(owners):
    side = 8 if owners == 128 else 2
    return side, side


def iota(shape, axis):
    return lax.broadcasted_iota(I32, shape, axis)


def kernel(
    cfg,
    hidden_ref, gain_ref, w1_ref, w2_ref, codes_ref, codes_t_ref, book_ref, embed_ref, size_ref,
    resid_out, cluster_out, avg_out, new_out,
    hid, book, embed, w1, w2, outv, avgv, newv,
    flat8, book8, r8, tot8, onehot, idxexp,
    table, items, slots, zgot, ysrc, ygot, want, picked, xcount,
    items_s, slots_s, want_s,
    qsend0, qsend1, qsend2, qrecv0, qrecv1, qrecv2,
    rsend0, rsend1, rsend2, rrecv0, rrecv1, rrecv2,
    xsum0, xsum1, xsum2,
    lsem, ssem, zsend, zrecv, ysend, yrecv, wsend, wrecv, fsend, frecv,
    qss, qrs, rss, rrs, xss, xrs, css, crs, osem,
):
    ny, nz, nx, rows, levels, code_dev = cfg
    owners = ny * nz * CORES
    nyc = ny * CORES
    width = nz * 16
    qsend, qrecv = (qsend0, qsend1, qsend2), (qrecv0, qrecv1, qrecv2)
    rsend, rrecv = (rsend0, rsend1, rsend2), (rrecv0, rrecv1, rrecv2)
    xsum = (xsum0, xsum1, xsum2)
    me = lax.axis_index("code")
    xi = lax.axis_index("item")
    core = me % CORES
    z = (me // CORES) % nz
    y = me // (CORES * nz)
    yc = y * CORES + core
    sibling = me + 1 - 2 * core

    def code_id(ty, tz, tc):
        return (ty * nz + tz) * CORES + tc

    def zmate(k):
        tz = (z + k) % nz
        return tz, code_id(y, tz, core)

    def ymate(k):
        tc = (core + k) % CORES
        ty = (y + k // CORES) % ny
        return ty, tc, code_id(ty, z, tc)

    def partner(k):
        d = k // CORES
        dz = d % nz
        tc = (core + k) % CORES
        tz = (z + dz) % nz
        ty = (y + dz + d // nz) % ny
        return code_id(ty, tz, tc), (ty * CORES + tc), tz

    def loop(low, high, step, unroll=1):
        def go(k, _):
            step(k)
            return 0

        lax.fori_loop(low, high, go, 0, unroll=unroll)

    def wait_bytes(view, sem):
        pltpu.make_async_copy(view, view, sem).wait()

    loads = [
        pltpu.make_async_copy(hidden_ref, hid, lsem.at[0]),
        pltpu.make_async_copy(book_ref, book, lsem.at[1]),
        pltpu.make_async_copy(w1_ref, w1.at[xi], lsem.at[2]),
        pltpu.make_async_copy(w2_ref, w2.at[xi], lsem.at[3]),
        pltpu.make_async_copy(embed_ref, embed, lsem.at[4]),
    ]
    for one in loads:
        one.start()

    barrier = pltpu.get_barrier_semaphore()

    def greet(device):
        pl.semaphore_signal(barrier, inc=1, device_id=device, device_id_type=MESH)

    loop(1, nz, lambda k: greet({"code": zmate(k)[1]}))
    loop(1, nyc, lambda k: greet({"code": ymate(k)[2]}))
    for d in range(1, nx):
        greet({"item": (xi + d) % nx})

    lane = iota((rows, LANES), 1)
    down, across = iota((rows, rows), 0), iota((rows, rows), 1)
    to_lane = iota((owners, LANES), 1)
    to_sub = iota((owners, rows), 0)
    requests = jnp.zeros((owners, LANES), I32)
    items[...] = jnp.zeros(items.shape, I32)
    slots[...] = jnp.zeros(slots.shape, I32)
    for level in range(levels):
        code_col, code_row = codes_ref[:, level : level + 1], codes_t_ref[level : level + 1, :]
        owner_col, owner_row = code_col // code_dev, code_row // code_dev
        same = owner_col == owner_row
        rank_row = jnp.sum(jnp.where(same & (down < across), 1, 0), axis=0, keepdims=True)
        rank_col = jnp.sum(jnp.where(same & (across < down), 1, 0), axis=1, keepdims=True)
        slots[level : level + 1, :rows] = owner_row
        slots[levels + level : levels + level + 1, :rows] = rank_row
        ring = owner_row // CORES % nz * nyc + owner_row // (CORES * nz) * CORES + owner_row % CORES
        for k in range(2):
            at = 2 * level + k
            chosen = jnp.where((to_sub == ring) & (rank_row == k), code_row % code_dev + 1, 0)
            local = jnp.sum(chosen, axis=1, keepdims=True)
            requests = jnp.where(to_lane == z * 8 + at, local, requests)
            number = jnp.where((lane == owner_col) & (rank_col == k), iota((rows, LANES), 0), 0)
            items[at : at + 1, :] = jnp.sum(number, axis=0, keepdims=True)
    table[...] = requests
    to_smem = [
        pltpu.make_async_copy(items, items_s, ssem.at[0]),
        pltpu.make_async_copy(slots, slots_s, ssem.at[1]),
    ]
    for one in to_smem:
        one.start()

    loads[0].wait()
    values = hid[...].astype(F32)
    power = jnp.mean(values * values, axis=-1, keepdims=True)
    normed = (values * lax.rsqrt(power + norm_eps) * gain_ref[...].astype(F32)).astype(BF16)
    hid[...] = normed
    loads[1].wait()
    for level in range(levels):
        for c in range(CHUNKS):
            flat8[pl.ds(c, code_dev, stride=CHUNKS), :] = book[level, :, c * LANES : (c + 1) * LANES]
        book8[level] = flat8[: code_dev * CHUNKS, :].reshape(code_dev, CHUNKS, LANES)
    for one in loads[2:]:
        one.wait()

    pl.semaphore_wait(barrier, nz - 1 + nyc - 1 + nx - 1)

    def ring_rows(tz):
        return pl.ds(pl.multiple_of(tz * nyc, nyc), nyc)

    def send_table(k):
        tz, device = zmate(k)
        pltpu.make_async_remote_copy(
            src_ref=table.at[ring_rows(tz)], dst_ref=zgot.at[z], send_sem=zsend, recv_sem=zrecv,
            device_id={"code": device}, device_id_type=MESH,
        ).start()

    loop(1, nz, send_table)
    zgot[z] = table[ring_rows(z), :]

    half = w1.shape[1] // CORES
    weights = (w1, w2)

    def part(w, source, which):
        return w.at[source, pl.ds(pl.multiple_of(which * half, half), half)]

    def weight_copy(i, d):
        return pltpu.make_async_remote_copy(
            src_ref=part(weights[i], xi, core), dst_ref=part(weights[i], xi, core),
            send_sem=wsend.at[i, d - 1], recv_sem=wrecv.at[i, d - 1],
            device_id={"item": (xi + d) % nx}, device_id_type=MESH,
        )

    def pass_on(i, d):
        source = (xi + nx - d) % nx
        return pltpu.make_async_remote_copy(
            src_ref=part(weights[i], source, core), dst_ref=part(weights[i], source, core),
            send_sem=fsend.at[i, d - 1], recv_sem=frecv.at[i, d - 1],
            device_id={"code": sibling}, device_id_type=MESH,
        )

    for i in range(2):
        for d in range(1, nx):
            weight_copy(i, d).start()

    wait_bytes(zgot.at[pl.ds(0, nz - 1)], zrecv)
    gathered = zgot[0]
    for s in range(1, nz):
        gathered = gathered + zgot[s]
    ysrc[:nyc, :] = gathered

    def tile_of(at):
        return pl.ds(pl.multiple_of(at // 8 * 8, 8), 8)

    def send_requests(k):
        ty, tc, device = ymate(k)
        pltpu.make_async_remote_copy(
            src_ref=ysrc.at[tile_of(ty * CORES + tc)], dst_ref=ygot.at[yc], send_sem=ysend, recv_sem=yrecv,
            device_id={"code": device}, device_id_type=MESH,
        ).start()

    loop(1, nyc, send_requests)
    ygot[yc] = ysrc[tile_of(yc), :]
    for one in to_smem:
        one.wait()
    wait_bytes(ygot.at[pl.ds(0, nyc - 1)], yrecv)
    mine = iota((nyc, 8, LANES), 1) == yc % 8
    want[...] = jnp.sum(jnp.where(mine, ygot[...], 0), axis=1) - 1
    picked[...] = jnp.maximum(want[...], 0)
    ask = pltpu.make_async_copy(picked, want_s, ssem.at[2])
    ask.start()

    code_row = iota((code_dev, LANES), 0)
    code_lane = iota((code_dev, LANES), 1)
    hist = jnp.zeros((code_dev, LANES), F32)
    for s in range(nyc):
        hist = hist + (want[s : s + 1, :] == code_row).astype(F32)
    xcount[xi] = jnp.zeros((8, LANES), F32)
    for level in range(levels):
        column = jnp.sum(
            jnp.where((code_lane % 8) // 2 == level, hist, 0.0), axis=1, keepdims=True
        )
        xcount[xi, level : level + 1, :] = jnp.sum(
            jnp.where(code_row == code_lane, column, 0.0), axis=0, keepdims=True
        )
    count_copies = [
        pltpu.make_async_remote_copy(
            src_ref=xcount.at[xi], dst_ref=xcount.at[xi], send_sem=css.at[d - 1], recv_sem=crs.at[d - 1],
            device_id={"item": (xi + d) % nx}, device_id_type=MESH,
        )
        for d in range(1, nx)
    ]
    ask.wait()

    def reply(level):
        def block(rs):
            rows_of = [book8[level, want_s[rs[0], rs[1] * 8 + 2 * level + k]] for k in range(2)]
            return jnp.concatenate(rows_of, axis=0).astype(BF16)

        qrecv[level][me] = block((yc, z))

        def one(k):
            device, tyc, tz = partner(k)
            qsend[level][device] = block((tyc, tz))
            pltpu.make_async_remote_copy(
                src_ref=qsend[level].at[device], dst_ref=qrecv[level].at[me],
                send_sem=qss.at[level], recv_sem=qrs.at[level],
                device_id={"code": device}, device_id_type=MESH,
            ).start()

        loop(1, owners, one)

    def send_rows(level):
        def block(owner):
            rows_of = [r8[items_s[2 * level + k, owner]] for k in range(2)]
            return jnp.concatenate(rows_of, axis=0).astype(BF16)

        rrecv[level][yc * nz + z] = block(me)

        def one(k):
            device, _, _ = partner(k)
            rsend[level][device] = block(device)
            pltpu.make_async_remote_copy(
                src_ref=rsend[level].at[device], dst_ref=rrecv[level].at[yc * nz + z],
                send_sem=rss.at[level], recv_sem=rrs.at[level],
                device_id={"code": device}, device_id_type=MESH,
            ).start()

        loop(1, owners, one)

    def subtract(level):
        wait_bytes(qrecv[level].at[pl.ds(0, owners - 1)], qrs.at[level])

        def one(i):
            second = slots_s[levels + level, i].astype(F32)
            pair = qrecv[level][slots_s[level, i]].astype(F32)
            r8[i] = r8[i] - (pair[:CHUNKS] * (1.0 - second) + pair[CHUNKS:] * second)

        loop(0, rows, one, unroll=4)

    reply(0)
    for one in count_copies:
        one.start()
    for d in range(1, nx):
        weight_copy(0, d).wait_recv()
        pass_on(0, d).start()
    reply(1)
    for d in range(1, nx):
        weight_copy(1, d).wait_recv()
        pass_on(1, d).start()

    depth = w1.shape[1] * nx
    for d in range(1, nx):
        pass_on(0, d).wait_recv()
    pre = jnp.dot(hid[...], w1[...].reshape(depth, -1), preferred_element_type=F32)
    middle = (pre / (1.0 + jnp.exp(-pre))).astype(BF16)
    for d in range(1, nx):
        pass_on(1, d).wait_recv()
    first = jnp.dot(middle, w2[...].reshape(depth, -1), preferred_element_type=F32)
    for c in range(CHUNKS):
        flat8[pl.ds(c, rows, stride=CHUNKS), :] = first[:, c * LANES : (c + 1) * LANES]
    r8[...] = flat8[: rows * CHUNKS, :].reshape(rows, CHUNKS, LANES)

    def sum_copy(level, d):
        return pltpu.make_async_remote_copy(
            src_ref=xsum[level].at[xi], dst_ref=xsum[level].at[xi],
            send_sem=xss.at[level, d - 1], recv_sem=xrs.at[level, d - 1],
            device_id={"item": (xi + d) % nx}, device_id_type=MESH,
        )

    def add_up(level):
        spread_from = iota((LANES, width), 0)
        spread_to = iota((LANES, width), 1)
        spread = (spread_from == (spread_to // 16) * 8 + 2 * level + (spread_to % 16) // 8).astype(BF16)
        asked = jnp.dot(want[...].astype(F32).astype(BF16), spread, preferred_element_type=F32)
        idxexp[...] = asked.astype(I32) * CHUNKS + iota((nyc, width), 1) % CHUNKS
        sum_rows = iota((code_dev * CHUNKS, width), 0)
        for s in range(nyc):
            onehot[:, s * width : (s + 1) * width] = (sum_rows == idxexp[s : s + 1, :]).astype(F32).astype(BF16)
        wait_bytes(rrecv[level].at[pl.ds(0, owners - 1)], rrs.at[level])
        got = rrecv[level][...].reshape(owners * 16, LANES)
        sums = jnp.dot(onehot[...], got, preferred_element_type=F32)
        xsum[level][xi] = sums.astype(BF16)
        for d in range(1, nx):
            sum_copy(level, d).start()

    def out_copies(level):
        return (
            pltpu.make_async_copy(avgv.at[level], avg_out.at[level], osem.at[level]),
            pltpu.make_async_copy(newv.at[level], new_out.at[level], osem.at[levels + level]),
        )

    def update(level):
        for d in range(1, nx):
            sum_copy(level, d).wait_recv()
        total = xsum[level][0].astype(F32)
        for x in range(1, nx):
            total = total + xsum[level][x].astype(F32)
        tot8[...] = total
        row = cluster_out[level : level + 1, :]
        same = iota((code_dev, code_dev), 0) == iota((code_dev, code_dev), 1)
        column = jnp.sum(jnp.where(same, row, 0.0), axis=1, keepdims=True)
        for c in range(CHUNKS):
            span = slice(c * LANES, (c + 1) * LANES)
            part_sum = tot8[pl.ds(c, code_dev, stride=CHUNKS), :]
            average = ema_decay * embed[level, :, span] + (1.0 - ema_decay) * part_sum
            avgv[level, :, span] = average
            newv[level, :, span] = average / column
        for one in out_copies(level):
            one.start()

    send_rows(0)
    subtract(0)
    send_rows(1)
    subtract(1)
    send_rows(2)
    for one in count_copies:
        one.wait_recv()
    counts = xcount[0]
    for x in range(1, nx):
        counts = counts + xcount[x]
    cluster_out[...] = ema_decay * size_ref[...] + (1.0 - ema_decay) * counts[:levels, :code_dev]
    add_up(0)
    reply(2)
    add_up(1)
    update(0)
    add_up(2)
    update(1)
    update(2)
    subtract(2)
    flat8[: rows * CHUNKS, :] = r8[...].reshape(rows * CHUNKS, LANES)
    for c in range(CHUNKS):
        outv[:, c * LANES : (c + 1) * LANES] = flat8[pl.ds(c, rows, stride=CHUNKS), :].astype(BF16)
    last = pltpu.make_async_copy(outv, resid_out, osem.at[2 * levels])
    last.start()

    wait_bytes(zgot.at[pl.ds(0, nz - 1)], zsend)
    wait_bytes(ygot.at[pl.ds(0, nyc - 1)], ysend)
    for d in range(1, nx):
        for i in range(2):
            weight_copy(i, d).wait_send()
            pass_on(i, d).wait_send()
        count_copies[d - 1].wait_send()
        for level in range(levels):
            sum_copy(level, d).wait_send()
    for level in range(levels):
        wait_bytes(qrecv[level].at[pl.ds(0, owners - 1)], qss.at[level])
        wait_bytes(rrecv[level].at[pl.ds(0, owners - 1)], rss.at[level])
        for one in out_copies(level):
            one.wait()
    last.wait()


def body(hidden, norm_gain, first_weight, second_weight, codes, codebook, embed_avg, cluster_size):
    rows, width = hidden.shape
    owners = lax.axis_size("code")
    nx = lax.axis_size("item")
    levels, code_dev, _ = codebook.shape
    ny, nz = grid_of(owners)
    nyc = ny * CORES
    cfg = (ny, nz, nx, rows, levels, code_dev)
    vmem, dma = pltpu.VMEM, pltpu.SemaphoreType.DMA
    blocks = [vmem((owners, 16, LANES), BF16)] * 12
    anywhere = pl.BlockSpec(memory_space=pl.ANY)
    inside = pl.BlockSpec(memory_space=pltpu.VMEM)
    shapes = (
        jax.ShapeDtypeStruct((rows, width), BF16),
        jax.ShapeDtypeStruct((levels, code_dev), F32),
        jax.ShapeDtypeStruct((levels, code_dev, width), F32),
        jax.ShapeDtypeStruct((levels, code_dev, width), F32),
    )
    return pl.pallas_call(
        functools.partial(kernel, cfg),
        out_shape=shapes,
        in_specs=[anywhere, inside, anywhere, anywhere, inside, inside, anywhere, anywhere, inside],
        out_specs=(anywhere, inside, anywhere, anywhere),
        scratch_shapes=[
            vmem((rows, width), BF16),
            vmem((levels, code_dev, width), F32),
            vmem((levels, code_dev, width), F32),
            vmem((nx,) + first_weight.shape, BF16),
            vmem((nx,) + second_weight.shape, BF16),
            vmem((rows, width), BF16),
            vmem((levels, code_dev, width), F32),
            vmem((levels, code_dev, width), F32),
            vmem((max(rows, code_dev) * CHUNKS, LANES), F32),
            vmem((levels, code_dev, CHUNKS, LANES), F32),
            vmem((rows, CHUNKS, LANES), F32),
            vmem((code_dev * CHUNKS, LANES), F32),
            vmem((code_dev * CHUNKS, owners * 16), BF16),
            vmem((nyc, nz * 16), I32),
            vmem((owners, LANES), I32),
            vmem((8, LANES), I32),
            vmem((8, LANES), I32),
            vmem((nz, nyc, LANES), I32),
            vmem((max(nyc, 8), LANES), I32),
            vmem((nyc, 8, LANES), I32),
            vmem((nyc, LANES), I32),
            vmem((nyc, LANES), I32),
            vmem((nx, 8, LANES), F32),
            pltpu.SMEM((8, LANES), I32),
            pltpu.SMEM((8, LANES), I32),
            pltpu.SMEM((nyc, LANES), I32),
            *blocks,
            *[vmem((nx, code_dev * CHUNKS, LANES), BF16)] * 3,
            dma((5,)),
            dma((3,)),
            dma,
            dma,
            dma,
            dma,
            dma((2, nx - 1)),
            dma((2, nx - 1)),
            dma((2, nx - 1)),
            dma((2, nx - 1)),
            dma((levels,)),
            dma((levels,)),
            dma((levels,)),
            dma((levels,)),
            dma((levels, nx - 1)),
            dma((levels, nx - 1)),
            dma((nx - 1,)),
            dma((nx - 1,)),
            dma((2 * levels + 1,)),
        ],
        compiler_params=pltpu.CompilerParams(
            collective_id=0, has_side_effects=True, vmem_limit_bytes=48 << 20
        ),
    )(
        hidden, norm_gain.reshape(1, width), first_weight, second_weight, codes, codes.T,
        codebook, embed_avg, cluster_size,
    )


def solution(mesh):
    in_specs = (
        P(("code", "item"), None),
        P(),
        P("item", None),
        P("item", None),
        P(("code", "item"), None),
        P(None, "code", None),
        P(None, "code", None),
        P(None, "code"),
    )
    out_specs = (
        P(("code", "item"), None),
        P(None, "code"),
        P(None, "code", None),
        P(None, "code", None),
    )
    return jax.shard_map(body, mesh=mesh, in_specs=in_specs, out_specs=out_specs, check_vma=False)
```

```python
import functools

import jax
import jax.numpy as jnp
from jax import lax
from jax.experimental import pallas as pl
from jax.experimental.pallas import tpu as pltpu
from jax.sharding import PartitionSpec as P

ema_decay = 0.8
norm_eps = 1e-06
MESH = pl.DeviceIdType.MESH
LANES = 128
CHUNKS = 8
CORES = 2
F32, BF16, I32 = jnp.float32, jnp.bfloat16, jnp.int32


def grid_of(owners):
    side = 8 if owners == 128 else 2
    return side, side


def iota(shape, axis):
    return lax.broadcasted_iota(I32, shape, axis)


def kernel(
    cfg,
    hidden_ref, gain_ref, w1_ref, w2_ref, codes_ref, book_ref, embed_ref, size_ref,
    resid_out, cluster_out, avg_out, new_out,
    hid, book, embed, w1, w2, outv, avgv, newv,
    flat8, book8, r8, tot8, onehot, idxexp,
    table, items, slots, zgot, ysrc, ygot, want, picked, xcount,
    items_s, slots_s, want_s,
    qsend0, qsend1, qsend2, qrecv0, qrecv1, qrecv2,
    rsend0, rsend1, rsend2, rrecv0, rrecv1, rrecv2,
    xsum0, xsum1, xsum2,
    lsem, ssem, zsend, zrecv, ysend, yrecv, wsend, wrecv, fsend, frecv,
    qss, qrs, rss, rrs, xss, xrs, css, crs, osem,
):
    ny, nz, nx, rows, levels, code_dev = cfg
    owners = ny * nz * CORES
    nyc = ny * CORES
    width = nz * 16
    qsend, qrecv = (qsend0, qsend1, qsend2), (qrecv0, qrecv1, qrecv2)
    rsend, rrecv = (rsend0, rsend1, rsend2), (rrecv0, rrecv1, rrecv2)
    xsum = (xsum0, xsum1, xsum2)
    me = lax.axis_index("code")
    xi = lax.axis_index("item")
    core = lax.rem(me, CORES)
    z = lax.rem(lax.div(me, CORES), nz)
    y = lax.div(me, CORES * nz)
    yc = y * CORES + core
    sibling = me + 1 - 2 * core
    cores = (core, 1 - core)
    columns = [lax.rem(z + a, nz) for a in range(nz)]

    def code_id(ty, tz, tc):
        return (ty * nz + tz) * CORES + tc

    zmates = [(columns[a], code_id(y, columns[a], core)) for a in range(1, nz)]
    ymates = [
        (lax.rem(y + a, ny) * CORES + cores[c], code_id(lax.rem(y + a, ny), z, cores[c]))
        for a in range(ny)
        for c in range(CORES)
        if (a, c) != (0, 0)
    ]

    def sweep(build, send, turn):
        def group(b, first=False):
            partners = []
            for a in range(nz):
                tz = columns[turn[0] * a % nz]
                ty = lax.rem(y + 2 * ny + turn[1] * (a + b), ny)
                for c in range(CORES):
                    if not (first and a == 0 and c == 0):
                        partners.append((code_id(ty, tz, cores[c]), ty * CORES + cores[c], tz))
            for one in partners:
                build(*one)
            for one in partners:
                send(one[0])

        group(0, first=True)
        loop(1, ny, group)

    def loop(low, high, step, unroll=1):
        def go(k, _):
            step(k)
            return 0

        lax.fori_loop(low, high, go, 0, unroll=unroll)

    def wait_bytes(view, sem):
        pltpu.make_async_copy(view, view, sem).wait()

    loads = [
        pltpu.make_async_copy(hidden_ref, hid, lsem.at[0]),
        pltpu.make_async_copy(book_ref, book, lsem.at[1]),
        pltpu.make_async_copy(w1_ref, w1.at[xi], lsem.at[2]),
        pltpu.make_async_copy(w2_ref, w2.at[xi], lsem.at[3]),
        pltpu.make_async_copy(embed_ref, embed, lsem.at[4]),
    ]
    for one in loads:
        one.start()

    barrier = pltpu.get_barrier_semaphore()

    def greet(device):
        pl.semaphore_signal(barrier, inc=1, device_id=device, device_id_type=MESH)

    for _, device in zmates + ymates:
        greet({"code": device})
    for d in range(1, nx):
        greet({"item": lax.rem(xi + d, nx)})

    lane = iota((rows, LANES), 1)
    down, across = iota((rows, rows), 0), iota((rows, rows), 1)
    to_lane = iota((owners, LANES), 1)
    to_sub = iota((owners, rows), 0)
    requests = jnp.zeros((owners, LANES), I32)
    items[...] = jnp.zeros(items.shape, I32)
    slots[...] = jnp.zeros(slots.shape, I32)
    for level in range(levels):
        code_row = codes_ref[level : level + 1, :]
        owner_row = code_row // code_dev
        owner_col = jnp.sum(jnp.where(down == across, owner_row, 0), axis=1, keepdims=True)
        same = owner_col == owner_row
        rank_row = jnp.sum(jnp.where(same & (down < across), 1, 0), axis=0, keepdims=True)
        rank_col = jnp.sum(jnp.where(same & (across < down), 1, 0), axis=1, keepdims=True)
        slots[level : level + 1, :rows] = owner_row
        slots[levels + level : levels + level + 1, :rows] = rank_row
        ring = owner_row // CORES % nz * nyc + owner_row // (CORES * nz) * CORES + owner_row % CORES
        for k in range(2):
            at = 2 * level + k
            chosen = jnp.where((to_sub == ring) & (rank_row == k), code_row % code_dev + 1, 0)
            local = jnp.sum(chosen, axis=1, keepdims=True)
            requests = jnp.where(to_lane == z * 8 + at, local, requests)
            number = jnp.where((lane == owner_col) & (rank_col == k), iota((rows, LANES), 0), 0)
            items[at : at + 1, :] = jnp.sum(number, axis=0, keepdims=True)
    table[...] = requests
    to_smem = [
        pltpu.make_async_copy(items, items_s, ssem.at[0]),
        pltpu.make_async_copy(slots, slots_s, ssem.at[1]),
    ]
    for one in to_smem:
        one.start()

    pl.semaphore_wait(barrier, nz - 1 + nyc - 1 + nx - 1)

    def ring_rows(tz):
        return pl.ds(pl.multiple_of(tz * nyc, nyc), nyc)

    for tz, device in zmates:
        pltpu.make_async_remote_copy(
            src_ref=table.at[ring_rows(tz)], dst_ref=zgot.at[z], send_sem=zsend, recv_sem=zrecv,
            device_id={"code": device}, device_id_type=MESH,
        ).start()

    zgot[z] = table[ring_rows(z), :]

    half = w1.shape[1] // CORES
    weights = (w1, w2)

    def part(w, source, which):
        return w.at[source, pl.ds(pl.multiple_of(which * half, half), half)]

    def weight_copy(i, d):
        return pltpu.make_async_remote_copy(
            src_ref=part(weights[i], xi, core), dst_ref=part(weights[i], xi, core),
            send_sem=wsend.at[i, d - 1], recv_sem=wrecv.at[i, d - 1],
            device_id={"item": lax.rem(xi + d, nx)}, device_id_type=MESH,
        )

    def pass_on(i, d):
        source = lax.rem(xi + nx - d, nx)
        return pltpu.make_async_remote_copy(
            src_ref=part(weights[i], source, core), dst_ref=part(weights[i], source, core),
            send_sem=fsend.at[i, d - 1], recv_sem=frecv.at[i, d - 1],
            device_id={"code": sibling}, device_id_type=MESH,
        )

    for i in range(2):
        loads[2 + i].wait()
        for d in range(1, nx):
            weight_copy(i, d).start()

    loads[1].wait()
    for level in range(levels):
        for c in range(CHUNKS):
            flat8[pl.ds(c, code_dev, stride=CHUNKS), :] = book[level, :, c * LANES : (c + 1) * LANES]
        book8[level] = flat8[: code_dev * CHUNKS, :].reshape(code_dev, CHUNKS, LANES)


    wait_bytes(zgot.at[pl.ds(0, nz - 1)], zrecv)
    gathered = zgot[0]
    for s in range(1, nz):
        gathered = gathered + zgot[s]
    ysrc[:nyc, :] = gathered

    def tile_of(at):
        return pl.ds(pl.multiple_of(lax.div(at, 8) * 8, 8), 8)

    for tyc, device in ymates:
        pltpu.make_async_remote_copy(
            src_ref=ysrc.at[tile_of(tyc)], dst_ref=ygot.at[yc], send_sem=ysend, recv_sem=yrecv,
            device_id={"code": device}, device_id_type=MESH,
        ).start()

    ygot[yc] = ysrc[tile_of(yc), :]
    for one in to_smem:
        one.wait()
    wait_bytes(ygot.at[pl.ds(0, nyc - 1)], yrecv)
    mine = iota((nyc, 8, LANES), 1) == lax.rem(yc, 8)
    want[...] = jnp.sum(jnp.where(mine, ygot[...], 0), axis=1) - 1
    picked[...] = jnp.maximum(want[...], 0)
    ask = pltpu.make_async_copy(picked, want_s, ssem.at[2])
    ask.start()

    code_row = iota((code_dev, LANES), 0)
    code_lane = iota((code_dev, LANES), 1)
    hist = jnp.zeros((code_dev, LANES), F32)
    for s in range(nyc):
        hist = hist + (want[s : s + 1, :] == code_row).astype(F32)
    xcount[xi] = jnp.zeros((8, LANES), F32)
    for level in range(levels):
        column = jnp.sum(
            jnp.where((code_lane % 8) // 2 == level, hist, 0.0), axis=1, keepdims=True
        )
        xcount[xi, level : level + 1, :] = jnp.sum(
            jnp.where(code_row == code_lane, column, 0.0), axis=0, keepdims=True
        )
    count_copies = [
        pltpu.make_async_remote_copy(
            src_ref=xcount.at[xi], dst_ref=xcount.at[xi], send_sem=css.at[d - 1], recv_sem=crs.at[d - 1],
            device_id={"item": lax.rem(xi + d, nx)}, device_id_type=MESH,
        )
        for d in range(1, nx)
    ]
    ask.wait()

    reply_turns = ((1, 1), (-1, -1), (-1, -1))
    row_turns = ((1, -1), (-1, 1), (1, 1))

    def reply(level):
        def block(tyc, tz):
            rows_of = [book8[level, want_s[tyc, tz * 8 + (2 * level + k)]] for k in range(2)]
            return jnp.concatenate(rows_of, axis=0).astype(BF16)

        def build(device, tyc, tz):
            qsend[level][device] = block(tyc, tz)

        def send(device):
            pltpu.make_async_remote_copy(
                src_ref=qsend[level].at[device], dst_ref=qrecv[level].at[me],
                send_sem=qss.at[level], recv_sem=qrs.at[level],
                device_id={"code": device}, device_id_type=MESH,
            ).start()

        qrecv[level][me] = block(yc, z)
        sweep(build, send, reply_turns[level])

    def send_rows(level):
        def block(owner):
            rows_of = [r8[items_s[2 * level + k, owner]] for k in range(2)]
            return jnp.concatenate(rows_of, axis=0).astype(BF16)

        def build(device, tyc, tz):
            rsend[level][device] = block(device)

        def send(device):
            pltpu.make_async_remote_copy(
                src_ref=rsend[level].at[device], dst_ref=rrecv[level].at[yc * nz + z],
                send_sem=rss.at[level], recv_sem=rrs.at[level],
                device_id={"code": device}, device_id_type=MESH,
            ).start()

        rrecv[level][yc * nz + z] = block(me)
        sweep(build, send, row_turns[level])

    def subtract(level):
        wait_bytes(qrecv[level].at[pl.ds(0, owners - 1)], qrs.at[level])

        def one(i):
            second = slots_s[levels + level, i].astype(F32)
            pair = qrecv[level][slots_s[level, i]].astype(F32)
            r8[i] = r8[i] - (pair[:CHUNKS] * (1.0 - second) + pair[CHUNKS:] * second)

        loop(0, rows, one, unroll=8)

    reply(0)
    for one in count_copies:
        one.start()
    for d in range(1, nx):
        weight_copy(0, d).wait_recv()
        pass_on(0, d).start()
    reply(1)
    for d in range(1, nx):
        weight_copy(1, d).wait_recv()
        pass_on(1, d).start()

    loads[0].wait()
    values = hid[...].astype(F32)
    power = jnp.mean(values * values, axis=-1, keepdims=True)
    scaled = values * lax.rsqrt(power + norm_eps)
    gain = gain_ref[...].astype(F32)
    for c in range(CHUNKS):
        span = slice(c * LANES, (c + 1) * LANES)
        hid[:, span] = (scaled[:, span] * gain[c : c + 1, :]).astype(BF16)

    depth = w1.shape[1] * nx
    for d in range(1, nx):
        pass_on(0, d).wait_recv()
    pre = jnp.dot(hid[...], w1[...].reshape(depth, -1), preferred_element_type=F32)
    middle = (pre / (1.0 + jnp.exp(-pre))).astype(BF16)
    for d in range(1, nx):
        pass_on(1, d).wait_recv()
    first = jnp.dot(middle, w2[...].reshape(depth, -1), preferred_element_type=F32)
    for c in range(CHUNKS):
        flat8[pl.ds(c, rows, stride=CHUNKS), :] = first[:, c * LANES : (c + 1) * LANES]
    r8[...] = flat8[: rows * CHUNKS, :].reshape(rows, CHUNKS, LANES)

    def sum_copy(level, d):
        return pltpu.make_async_remote_copy(
            src_ref=xsum[level].at[xi], dst_ref=xsum[level].at[xi],
            send_sem=xss.at[level, d - 1], recv_sem=xrs.at[level, d - 1],
            device_id={"item": lax.rem(xi + d, nx)}, device_id_type=MESH,
        )

    def add_up(level):
        spread_from = iota((LANES, width), 0)
        spread_to = iota((LANES, width), 1)
        spread = (spread_from == (spread_to // 16) * 8 + 2 * level + (spread_to % 16) // 8).astype(BF16)
        asked = jnp.dot(want[...].astype(F32).astype(BF16), spread, preferred_element_type=F32)
        idxexp[...] = asked.astype(I32) * CHUNKS + iota((nyc, width), 1) % CHUNKS
        sum_rows = iota((code_dev * CHUNKS, width), 0)
        for s in range(nyc):
            onehot[:, s * width : (s + 1) * width] = (sum_rows == idxexp[s : s + 1, :]).astype(F32).astype(BF16)
        wait_bytes(rrecv[level].at[pl.ds(0, owners - 1)], rrs.at[level])
        got = rrecv[level][...].reshape(owners * 16, LANES)
        sums = jnp.dot(onehot[...], got, preferred_element_type=F32)
        xsum[level][xi] = sums.astype(BF16)
        for d in range(1, nx):
            sum_copy(level, d).start()

    def out_copies(level):
        return (
            pltpu.make_async_copy(avgv.at[level], avg_out.at[level], osem.at[level]),
            pltpu.make_async_copy(newv.at[level], new_out.at[level], osem.at[levels + level]),
        )

    def update(level):
        for d in range(1, nx):
            sum_copy(level, d).wait_recv()
        total = xsum[level][0].astype(F32)
        for x in range(1, nx):
            total = total + xsum[level][x].astype(F32)
        tot8[...] = total
        row = cluster_out[level : level + 1, :]
        same = iota((code_dev, code_dev), 0) == iota((code_dev, code_dev), 1)
        column = jnp.sum(jnp.where(same, row, 0.0), axis=1, keepdims=True)
        for c in range(CHUNKS):
            span = slice(c * LANES, (c + 1) * LANES)
            part_sum = tot8[pl.ds(c, code_dev, stride=CHUNKS), :]
            average = ema_decay * embed[level, :, span] + (1.0 - ema_decay) * part_sum
            avgv[level, :, span] = average
            newv[level, :, span] = average / column
        for one in out_copies(level):
            one.start()

    loads[4].wait()
    send_rows(0)
    subtract(0)
    send_rows(1)
    subtract(1)
    send_rows(2)
    for one in count_copies:
        one.wait_recv()
    counts = xcount[0]
    for x in range(1, nx):
        counts = counts + xcount[x]
    cluster_out[...] = ema_decay * size_ref[...] + (1.0 - ema_decay) * counts[:levels, :code_dev]
    add_up(0)
    reply(2)
    add_up(1)
    update(0)
    add_up(2)
    update(1)
    update(2)
    subtract(2)
    flat8[: rows * CHUNKS, :] = r8[...].reshape(rows * CHUNKS, LANES)
    for c in range(CHUNKS):
        outv[:, c * LANES : (c + 1) * LANES] = flat8[pl.ds(c, rows, stride=CHUNKS), :].astype(BF16)
    last = pltpu.make_async_copy(outv, resid_out, osem.at[2 * levels])
    last.start()

    wait_bytes(zgot.at[pl.ds(0, nz - 1)], zsend)
    wait_bytes(ygot.at[pl.ds(0, nyc - 1)], ysend)
    for d in range(1, nx):
        for i in range(2):
            weight_copy(i, d).wait_send()
            pass_on(i, d).wait_send()
        count_copies[d - 1].wait_send()
        for level in range(levels):
            sum_copy(level, d).wait_send()
    for level in range(levels):
        wait_bytes(qrecv[level].at[pl.ds(0, owners - 1)], qss.at[level])
        wait_bytes(rrecv[level].at[pl.ds(0, owners - 1)], rss.at[level])
        for one in out_copies(level):
            one.wait()
    last.wait()


def body(hidden, norm_gain, first_weight, second_weight, codes, codebook, embed_avg, cluster_size):
    rows, width = hidden.shape
    owners = lax.axis_size("code")
    nx = lax.axis_size("item")
    levels, code_dev, _ = codebook.shape
    ny, nz = grid_of(owners)
    nyc = ny * CORES
    cfg = (ny, nz, nx, rows, levels, code_dev)
    vmem, dma = pltpu.VMEM, pltpu.SemaphoreType.DMA
    blocks = [vmem((owners, 16, LANES), BF16)] * 12
    anywhere = pl.BlockSpec(memory_space=pl.ANY)
    inside = pl.BlockSpec(memory_space=pltpu.VMEM)
    shapes = (
        jax.ShapeDtypeStruct((rows, width), BF16),
        jax.ShapeDtypeStruct((levels, code_dev), F32),
        jax.ShapeDtypeStruct((levels, code_dev, width), F32),
        jax.ShapeDtypeStruct((levels, code_dev, width), F32),
    )
    return pl.pallas_call(
        functools.partial(kernel, cfg),
        out_shape=shapes,
        in_specs=[anywhere, inside, anywhere, anywhere, inside, anywhere, anywhere, inside],
        out_specs=(anywhere, inside, anywhere, anywhere),
        scratch_shapes=[
            vmem((rows, width), BF16),
            vmem((levels, code_dev, width), F32),
            vmem((levels, code_dev, width), F32),
            vmem((nx,) + first_weight.shape, BF16),
            vmem((nx,) + second_weight.shape, BF16),
            vmem((rows, width), BF16),
            vmem((levels, code_dev, width), F32),
            vmem((levels, code_dev, width), F32),
            vmem((max(rows, code_dev) * CHUNKS, LANES), F32),
            vmem((levels, code_dev, CHUNKS, LANES), F32),
            vmem((rows, CHUNKS, LANES), F32),
            vmem((code_dev * CHUNKS, LANES), F32),
            vmem((code_dev * CHUNKS, owners * 16), BF16),
            vmem((nyc, nz * 16), I32),
            vmem((owners, LANES), I32),
            vmem((8, LANES), I32),
            vmem((8, LANES), I32),
            vmem((nz, nyc, LANES), I32),
            vmem((max(nyc, 8), LANES), I32),
            vmem((nyc, 8, LANES), I32),
            vmem((nyc, LANES), I32),
            vmem((nyc, LANES), I32),
            vmem((nx, 8, LANES), F32),
            pltpu.SMEM((8, LANES), I32),
            pltpu.SMEM((8, LANES), I32),
            pltpu.SMEM((nyc, LANES), I32),
            *blocks,
            *[vmem((nx, code_dev * CHUNKS, LANES), BF16)] * 3,
            dma((5,)),
            dma((3,)),
            dma,
            dma,
            dma,
            dma,
            dma((2, nx - 1)),
            dma((2, nx - 1)),
            dma((2, nx - 1)),
            dma((2, nx - 1)),
            dma((levels,)),
            dma((levels,)),
            dma((levels,)),
            dma((levels,)),
            dma((levels, nx - 1)),
            dma((levels, nx - 1)),
            dma((nx - 1,)),
            dma((nx - 1,)),
            dma((2 * levels + 1,)),
        ],
        compiler_params=pltpu.CompilerParams(
            collective_id=0, has_side_effects=True, vmem_limit_bytes=64 << 20
        ),
    )(
        hidden, norm_gain.reshape(CHUNKS, LANES), first_weight, second_weight, codes.T,
        codebook, embed_avg, cluster_size,
    )


def solution(mesh):
    in_specs = (
        P(("code", "item"), None),
        P(),
        P("item", None),
        P("item", None),
        P(("code", "item"), None),
        P(None, "code", None),
        P(None, "code", None),
        P(None, "code"),
    )
    out_specs = (
        P(("code", "item"), None),
        P(None, "code"),
        P(None, "code", None),
        P(None, "code", None),
    )
    return jax.shard_map(body, mesh=mesh, in_specs=in_specs, out_specs=out_specs, check_vma=False)
```

```python
import functools

import jax
import jax.numpy as jnp
from jax import lax
from jax.experimental import pallas as pl
from jax.experimental.pallas import tpu as pltpu
from jax.sharding import PartitionSpec as P

ema_decay = 0.8
norm_eps = 1e-06
MESH = pl.DeviceIdType.MESH
LANES = 128
CHUNKS = 8
CORES = 2
F32, BF16, I32 = jnp.float32, jnp.bfloat16, jnp.int32


def grid_of(owners):
    side = 8 if owners == 128 else 2
    return side, side


def iota(shape, axis):
    return lax.broadcasted_iota(I32, shape, axis)


def kernel(
    cfg,
    hidden_ref, gain_ref, w1_ref, w2_ref, codes_ref, book_ref, embed_ref, size_ref,
    resid_out, cluster_out, avg_out, new_out,
    hid, book, embed, w1, w2, outv, avgv, newv, cluster,
    flat8, book8, r8, tot8, onehot, idxexp,
    table, items, slots, zgot, ysrc, ygot, want, picked, xcount,
    items_s, slots_s, want_s,
    qsend0, qsend1, qsend2, qrecv0, qrecv1, qrecv2,
    rsend0, rsend1, rsend2, rrecv0, rrecv1, rrecv2,
    xsum0, xsum1, xsum2,
    lsem, ssem, zsend, zrecv, ysend, yrecv, wsend, wrecv, fsend, frecv,
    qss, qrs, rss, rrs, xss, xrs, css, crs, osem,
):
    ny, nz, nx, rows, levels, code_dev = cfg
    owners = ny * nz * CORES
    nyc = ny * CORES
    width = nz * 16
    qsend, qrecv = (qsend0, qsend1, qsend2), (qrecv0, qrecv1, qrecv2)
    rsend, rrecv = (rsend0, rsend1, rsend2), (rrecv0, rrecv1, rrecv2)
    xsum = (xsum0, xsum1, xsum2)
    me = lax.axis_index("code")
    xi = lax.axis_index("item")
    core = lax.rem(me, CORES)
    z = lax.rem(lax.div(me, CORES), nz)
    y = lax.div(me, CORES * nz)
    yc = y * CORES + core
    sibling = me + 1 - 2 * core
    cores = (core, 1 - core)
    columns = [lax.rem(z + a, nz) for a in range(nz)]

    def code_id(ty, tz, tc):
        return (ty * nz + tz) * CORES + tc

    zmates = [(columns[a], code_id(y, columns[a], core)) for a in range(1, nz)]
    ymates = [
        (lax.rem(y + a, ny) * CORES + cores[c], code_id(lax.rem(y + a, ny), z, cores[c]))
        for a in range(ny)
        for c in range(CORES)
        if (a, c) != (0, 0)
    ]

    def sweep(build, send, turn):
        def group(b, first=False):
            partners = []
            for a in range(nz):
                if turn[2]:
                    tz = lax.rem(z + 2 * nz + turn[0] * (a + b), nz)
                    ty = lax.rem(y + ny + turn[1] * a, ny)
                else:
                    tz = columns[turn[0] * a % nz]
                    ty = lax.rem(y + 2 * ny + turn[1] * (a + b), ny)
                for c in range(CORES):
                    if not (first and a == 0 and c == 0):
                        partners.append((code_id(ty, tz, cores[c]), ty * CORES + cores[c], tz))
            for one in partners:
                build(*one)
            for one in partners:
                send(one[0])

        group(0, first=True)
        loop(1, ny, group)

    def loop(low, high, step, unroll=1):
        def go(k, _):
            step(k)
            return 0

        lax.fori_loop(low, high, go, 0, unroll=unroll)

    def wait_bytes(view, sem):
        pltpu.make_async_copy(view, view, sem).wait()

    loads = [
        pltpu.make_async_copy(hidden_ref, hid, lsem.at[0]),
        pltpu.make_async_copy(book_ref, book, lsem.at[1]),
        pltpu.make_async_copy(w1_ref, w1.at[xi], lsem.at[2]),
        pltpu.make_async_copy(w2_ref, w2.at[xi], lsem.at[3]),
        pltpu.make_async_copy(embed_ref, embed, lsem.at[4]),
    ]
    for one in loads:
        one.start()

    barrier = pltpu.get_barrier_semaphore()

    def greet(device):
        pl.semaphore_signal(barrier, inc=1, device_id=device, device_id_type=MESH)

    for _, device in zmates + ymates:
        greet({"code": device})
    for d in range(1, nx):
        greet({"item": lax.rem(xi + d, nx)})

    lane = iota((rows, LANES), 1)
    down, across = iota((rows, rows), 0), iota((rows, rows), 1)
    to_lane = iota((owners, LANES), 1)
    to_sub = iota((owners, rows), 0)
    requests = jnp.zeros((owners, LANES), I32)
    items[...] = jnp.zeros(items.shape, I32)
    slots[...] = jnp.zeros(slots.shape, I32)
    for level in range(levels):
        code_row = codes_ref[level : level + 1, :]
        owner_row = code_row // code_dev
        owner_col = jnp.sum(jnp.where(down == across, owner_row, 0), axis=1, keepdims=True)
        same = owner_col == owner_row
        rank_row = jnp.sum(jnp.where(same & (down < across), 1, 0), axis=0, keepdims=True)
        rank_col = jnp.sum(jnp.where(same & (across < down), 1, 0), axis=1, keepdims=True)
        slots[level : level + 1, :rows] = owner_row
        slots[levels + level : levels + level + 1, :rows] = rank_row
        ring = owner_row // CORES % nz * nyc + owner_row // (CORES * nz) * CORES + owner_row % CORES
        for k in range(2):
            at = 2 * level + k
            chosen = jnp.where((to_sub == ring) & (rank_row == k), code_row % code_dev + 1, 0)
            local = jnp.sum(chosen, axis=1, keepdims=True)
            requests = jnp.where(to_lane == z * 8 + at, local, requests)
            number = jnp.where((lane == owner_col) & (rank_col == k), iota((rows, LANES), 0), 0)
            items[at : at + 1, :] = jnp.sum(number, axis=0, keepdims=True)
    table[...] = requests
    to_smem = [
        pltpu.make_async_copy(items, items_s, ssem.at[0]),
        pltpu.make_async_copy(slots, slots_s, ssem.at[1]),
    ]
    for one in to_smem:
        one.start()

    pl.semaphore_wait(barrier, nz - 1 + nyc - 1 + nx - 1)

    def ring_rows(tz):
        return pl.ds(pl.multiple_of(tz * nyc, nyc), nyc)

    for tz, device in zmates:
        pltpu.make_async_remote_copy(
            src_ref=table.at[ring_rows(tz)], dst_ref=zgot.at[z], send_sem=zsend, recv_sem=zrecv,
            device_id={"code": device}, device_id_type=MESH,
        ).start()

    zgot[z] = table[ring_rows(z), :]

    half = w1.shape[1] // CORES
    weights = (w1, w2)

    def part(w, source, which):
        return w.at[source, pl.ds(pl.multiple_of(which * half, half), half)]

    def weight_copy(i, d):
        return pltpu.make_async_remote_copy(
            src_ref=part(weights[i], xi, core), dst_ref=part(weights[i], xi, core),
            send_sem=wsend.at[i, d - 1], recv_sem=wrecv.at[i, d - 1],
            device_id={"item": lax.rem(xi + d, nx)}, device_id_type=MESH,
        )

    def pass_on(i, d):
        source = lax.rem(xi + nx - d, nx)
        return pltpu.make_async_remote_copy(
            src_ref=part(weights[i], source, core), dst_ref=part(weights[i], source, core),
            send_sem=fsend.at[i, d - 1], recv_sem=frecv.at[i, d - 1],
            device_id={"code": sibling}, device_id_type=MESH,
        )

    for i in range(2):
        loads[2 + i].wait()
        for d in range(1, nx):
            weight_copy(i, d).start()

    loads[1].wait()
    for level in range(levels):
        for c in range(CHUNKS):
            flat8[pl.ds(c, code_dev, stride=CHUNKS), :] = book[level, :, c * LANES : (c + 1) * LANES]
        book8[level] = flat8[: code_dev * CHUNKS, :].reshape(code_dev, CHUNKS, LANES)


    wait_bytes(zgot.at[pl.ds(0, nz - 1)], zrecv)
    gathered = zgot[0]
    for s in range(1, nz):
        gathered = gathered + zgot[s]
    ysrc[:nyc, :] = gathered

    def tile_of(at):
        return pl.ds(pl.multiple_of(lax.div(at, 8) * 8, 8), 8)

    for tyc, device in ymates:
        pltpu.make_async_remote_copy(
            src_ref=ysrc.at[tile_of(tyc)], dst_ref=ygot.at[yc], send_sem=ysend, recv_sem=yrecv,
            device_id={"code": device}, device_id_type=MESH,
        ).start()

    ygot[yc] = ysrc[tile_of(yc), :]
    for one in to_smem:
        one.wait()
    wait_bytes(ygot.at[pl.ds(0, nyc - 1)], yrecv)
    mine = iota((nyc, 8, LANES), 1) == lax.rem(yc, 8)
    want[...] = jnp.sum(jnp.where(mine, ygot[...], 0), axis=1) - 1
    picked[...] = jnp.maximum(want[...], 0)
    ask = pltpu.make_async_copy(picked, want_s, ssem.at[2])
    ask.start()

    code_row = iota((code_dev, LANES), 0)
    code_lane = iota((code_dev, LANES), 1)
    hist = jnp.zeros((code_dev, LANES), F32)
    for s in range(nyc):
        hist = hist + (want[s : s + 1, :] == code_row).astype(F32)
    xcount[xi] = jnp.zeros((8, LANES), F32)
    for level in range(levels):
        column = jnp.sum(
            jnp.where((code_lane % 8) // 2 == level, hist, 0.0), axis=1, keepdims=True
        )
        xcount[xi, level : level + 1, :] = jnp.sum(
            jnp.where(code_row == code_lane, column, 0.0), axis=0, keepdims=True
        )
    count_copies = [
        pltpu.make_async_remote_copy(
            src_ref=xcount.at[xi], dst_ref=xcount.at[xi], send_sem=css.at[d - 1], recv_sem=crs.at[d - 1],
            device_id={"item": lax.rem(xi + d, nx)}, device_id_type=MESH,
        )
        for d in range(1, nx)
    ]
    ask.wait()

    reply_turns = ((1, 1, 0), (-1, -1, 1), (1, -1, 1))
    row_turns = ((1, -1, 0), (-1, 1, 1), (-1, -1, 0))

    def reply(level):
        def block(tyc, tz):
            rows_of = [book8[level, want_s[tyc, tz * 8 + (2 * level + k)]] for k in range(2)]
            return jnp.concatenate(rows_of, axis=0).astype(BF16)

        def build(device, tyc, tz):
            qsend[level][device] = block(tyc, tz)

        def send(device):
            pltpu.make_async_remote_copy(
                src_ref=qsend[level].at[device], dst_ref=qrecv[level].at[me],
                send_sem=qss.at[level], recv_sem=qrs.at[level],
                device_id={"code": device}, device_id_type=MESH,
            ).start()

        qrecv[level][me] = block(yc, z)
        sweep(build, send, reply_turns[level])

    def send_rows(level):
        def block(owner):
            rows_of = [r8[items_s[2 * level + k, owner]] for k in range(2)]
            return jnp.concatenate(rows_of, axis=0).astype(BF16)

        def build(device, tyc, tz):
            rsend[level][device] = block(device)

        def send(device):
            pltpu.make_async_remote_copy(
                src_ref=rsend[level].at[device], dst_ref=rrecv[level].at[yc * nz + z],
                send_sem=rss.at[level], recv_sem=rrs.at[level],
                device_id={"code": device}, device_id_type=MESH,
            ).start()

        rrecv[level][yc * nz + z] = block(me)
        sweep(build, send, row_turns[level])

    def subtract(level):
        wait_bytes(qrecv[level].at[pl.ds(0, owners - 1)], qrs.at[level])

        def one(i):
            second = slots_s[levels + level, i].astype(F32)
            pair = qrecv[level][slots_s[level, i]].astype(F32)
            r8[i] = r8[i] - (pair[:CHUNKS] * (1.0 - second) + pair[CHUNKS:] * second)

        loop(0, rows, one, unroll=8)

    reply(0)
    for one in count_copies:
        one.start()
    for d in range(1, nx):
        weight_copy(0, d).wait_recv()
        pass_on(0, d).start()
    reply(1)
    for d in range(1, nx):
        weight_copy(1, d).wait_recv()
        pass_on(1, d).start()

    loads[0].wait()
    values = hid[...].astype(F32)
    power = jnp.mean(values * values, axis=-1, keepdims=True)
    scaled = values * lax.rsqrt(power + norm_eps)
    gain = gain_ref[...].astype(F32)
    for c in range(CHUNKS):
        span = slice(c * LANES, (c + 1) * LANES)
        hid[:, span] = (scaled[:, span] * gain[c : c + 1, :]).astype(BF16)

    depth = w1.shape[1] * nx
    for d in range(1, nx):
        pass_on(0, d).wait_recv()
    pre = jnp.dot(hid[...], w1[...].reshape(depth, -1), preferred_element_type=F32)
    middle = (pre / (1.0 + jnp.exp(-pre))).astype(BF16)
    for d in range(1, nx):
        pass_on(1, d).wait_recv()
    first = jnp.dot(middle, w2[...].reshape(depth, -1), preferred_element_type=F32)
    for c in range(CHUNKS):
        flat8[pl.ds(c, rows, stride=CHUNKS), :] = first[:, c * LANES : (c + 1) * LANES]
    r8[...] = flat8[: rows * CHUNKS, :].reshape(rows, CHUNKS, LANES)

    def sum_copy(level, d):
        return pltpu.make_async_remote_copy(
            src_ref=xsum[level].at[xi], dst_ref=xsum[level].at[xi],
            send_sem=xss.at[level, d - 1], recv_sem=xrs.at[level, d - 1],
            device_id={"item": lax.rem(xi + d, nx)}, device_id_type=MESH,
        )

    def add_up(level):
        spread_from = iota((LANES, width), 0)
        spread_to = iota((LANES, width), 1)
        spread = (spread_from == (spread_to // 16) * 8 + 2 * level + (spread_to % 16) // 8).astype(BF16)
        asked = jnp.dot(want[...].astype(F32).astype(BF16), spread, preferred_element_type=F32)
        idxexp[...] = asked.astype(I32) * CHUNKS + iota((nyc, width), 1) % CHUNKS
        sum_rows = iota((code_dev * CHUNKS, width), 0)
        for s in range(nyc):
            onehot[:, s * width : (s + 1) * width] = (sum_rows == idxexp[s : s + 1, :]).astype(F32).astype(BF16)
        wait_bytes(rrecv[level].at[pl.ds(0, owners - 1)], rrs.at[level])
        got = rrecv[level][...].reshape(owners * 16, LANES)
        sums = jnp.dot(onehot[...], got, preferred_element_type=F32)
        xsum[level][xi] = sums.astype(BF16)
        for d in range(1, nx):
            sum_copy(level, d).start()

    def out_copies(level):
        return (
            pltpu.make_async_copy(avgv.at[level], avg_out.at[level], osem.at[level]),
            pltpu.make_async_copy(newv.at[level], new_out.at[level], osem.at[levels + level]),
        )

    def update(level):
        for d in range(1, nx):
            sum_copy(level, d).wait_recv()
        total = xsum[level][0].astype(F32)
        for x in range(1, nx):
            total = total + xsum[level][x].astype(F32)
        tot8[...] = total
        row = cluster[level : level + 1, :]
        same = iota((code_dev, code_dev), 0) == iota((code_dev, code_dev), 1)
        column = jnp.sum(jnp.where(same, row, 0.0), axis=1, keepdims=True)
        for c in range(CHUNKS):
            span = slice(c * LANES, (c + 1) * LANES)
            part_sum = tot8[pl.ds(c, code_dev, stride=CHUNKS), :]
            average = ema_decay * embed[level, :, span] + (1.0 - ema_decay) * part_sum
            avgv[level, :, span] = average
            newv[level, :, span] = average / column
        for one in out_copies(level):
            one.start()

    loads[4].wait()
    send_rows(0)
    subtract(0)
    send_rows(1)
    subtract(1)
    send_rows(2)
    for one in count_copies:
        one.wait_recv()
    counts = xcount[0]
    for x in range(1, nx):
        counts = counts + xcount[x]
    cluster[...] = ema_decay * size_ref[...] + (1.0 - ema_decay) * counts[:levels, :code_dev]
    cluster_copy = pltpu.make_async_copy(cluster, cluster_out, lsem.at[0])
    cluster_copy.start()
    add_up(0)
    reply(2)
    add_up(1)
    update(0)
    add_up(2)
    update(1)
    update(2)
    subtract(2)
    flat8[: rows * CHUNKS, :] = r8[...].reshape(rows * CHUNKS, LANES)
    for c in range(CHUNKS):
        outv[:, c * LANES : (c + 1) * LANES] = flat8[pl.ds(c, rows, stride=CHUNKS), :].astype(BF16)
    last = pltpu.make_async_copy(outv, resid_out, osem.at[2 * levels])
    last.start()

    wait_bytes(zgot.at[pl.ds(0, nz - 1)], zsend)
    wait_bytes(ygot.at[pl.ds(0, nyc - 1)], ysend)
    for d in range(1, nx):
        for i in range(2):
            weight_copy(i, d).wait_send()
            pass_on(i, d).wait_send()
        count_copies[d - 1].wait_send()
        for level in range(levels):
            sum_copy(level, d).wait_send()
    for level in range(levels):
        wait_bytes(qrecv[level].at[pl.ds(0, owners - 1)], qss.at[level])
        wait_bytes(rrecv[level].at[pl.ds(0, owners - 1)], rss.at[level])
        for one in out_copies(level):
            one.wait()
    last.wait()
    cluster_copy.wait()


def settle(levels, *refs):
    sources, targets, held, came, went = refs[:4], refs[4:8], refs[8:12], refs[12], refs[13]
    views = [(sources[i], held[i], targets[i]) for i in (0, 1)]
    for level in range(levels):
        views += [(sources[i].at[level], held[i].at[level], targets[i].at[level]) for i in (2, 3)]
    loads = [pltpu.make_async_copy(a, b, came.at[i]) for i, (a, b, _) in enumerate(views)]
    stores = [pltpu.make_async_copy(b, c, went.at[i]) for i, (_, b, c) in enumerate(views)]
    for one in loads:
        one.start()
    for load, store in zip(loads, stores):
        load.wait()
        store.start()
    for one in stores:
        one.wait()


def body(hidden, norm_gain, first_weight, second_weight, codes, codebook, embed_avg, cluster_size):
    rows, width = hidden.shape
    owners = lax.axis_size("code")
    nx = lax.axis_size("item")
    levels, code_dev, _ = codebook.shape
    ny, nz = grid_of(owners)
    nyc = ny * CORES
    cfg = (ny, nz, nx, rows, levels, code_dev)
    vmem, dma = pltpu.VMEM, pltpu.SemaphoreType.DMA
    blocks = [vmem((owners, 16, LANES), BF16)] * 12
    anywhere = pl.BlockSpec(memory_space=pl.ANY)
    inside = pl.BlockSpec(memory_space=pltpu.VMEM)
    shapes = (
        jax.ShapeDtypeStruct((rows, width), BF16),
        jax.ShapeDtypeStruct((levels, code_dev), F32),
        jax.ShapeDtypeStruct((levels, code_dev, width), F32),
        jax.ShapeDtypeStruct((levels, code_dev, width), F32),
    )
    results = pl.pallas_call(
        functools.partial(kernel, cfg),
        out_shape=shapes,
        in_specs=[anywhere, inside, anywhere, anywhere, inside, anywhere, anywhere, inside],
        out_specs=(anywhere, anywhere, anywhere, anywhere),
        scratch_shapes=[
            vmem((rows, width), BF16),
            vmem((levels, code_dev, width), F32),
            vmem((levels, code_dev, width), F32),
            vmem((nx,) + first_weight.shape, BF16),
            vmem((nx,) + second_weight.shape, BF16),
            vmem((rows, width), BF16),
            vmem((levels, code_dev, width), F32),
            vmem((levels, code_dev, width), F32),
            vmem((levels, code_dev), F32),
            vmem((max(rows, code_dev) * CHUNKS, LANES), F32),
            vmem((levels, code_dev, CHUNKS, LANES), F32),
            vmem((rows, CHUNKS, LANES), F32),
            vmem((code_dev * CHUNKS, LANES), F32),
            vmem((code_dev * CHUNKS, owners * 16), BF16),
            vmem((nyc, nz * 16), I32),
            vmem((owners, LANES), I32),
            vmem((8, LANES), I32),
            vmem((8, LANES), I32),
            vmem((nz, nyc, LANES), I32),
            vmem((max(nyc, 8), LANES), I32),
            vmem((nyc, 8, LANES), I32),
            vmem((nyc, LANES), I32),
            vmem((nyc, LANES), I32),
            vmem((nx, 8, LANES), F32),
            pltpu.SMEM((8, LANES), I32),
            pltpu.SMEM((8, LANES), I32),
            pltpu.SMEM((nyc, LANES), I32),
            *blocks,
            *[vmem((nx, code_dev * CHUNKS, LANES), BF16)] * 3,
            dma((5,)),
            dma((3,)),
            dma,
            dma,
            dma,
            dma,
            dma((2, nx - 1)),
            dma((2, nx - 1)),
            dma((2, nx - 1)),
            dma((2, nx - 1)),
            dma((levels,)),
            dma((levels,)),
            dma((levels,)),
            dma((levels,)),
            dma((levels, nx - 1)),
            dma((levels, nx - 1)),
            dma((nx - 1,)),
            dma((nx - 1,)),
            dma((2 * levels + 1,)),
        ],
        compiler_params=pltpu.CompilerParams(
            collective_id=0, has_side_effects=True, vmem_limit_bytes=64 << 20
        ),
    )(
        hidden, norm_gain.reshape(CHUNKS, LANES), first_weight, second_weight, codes.T,
        codebook, embed_avg, cluster_size,
    )
    return pl.pallas_call(
        functools.partial(settle, levels),
        out_shape=shapes,
        in_specs=[anywhere] * 4,
        out_specs=(anywhere,) * 4,
        scratch_shapes=[vmem(x.shape, x.dtype) for x in shapes] + [dma((2 + 2 * levels,))] * 2,
        compiler_params=pltpu.CompilerParams(vmem_limit_bytes=64 << 20),
    )(*results)


def solution(mesh):
    in_specs = (
        P(("code", "item"), None),
        P(),
        P("item", None),
        P("item", None),
        P(("code", "item"), None),
        P(None, "code", None),
        P(None, "code", None),
        P(None, "code"),
    )
    out_specs = (
        P(("code", "item"), None),
        P(None, "code"),
        P(None, "code", None),
        P(None, "code", None),
    )
    return jax.shard_map(body, mesh=mesh, in_specs=in_specs, out_specs=out_specs, check_vma=False)
```

```python
import functools

import jax
import jax.numpy as jnp
from jax import lax
from jax.experimental import pallas as pl
from jax.experimental.pallas import tpu as pltpu
from jax.sharding import PartitionSpec as P

ema_decay = 0.8
norm_eps = 1e-06
MESH = pl.DeviceIdType.MESH
LANES = 128
CHUNKS = 8
CORES = 2
F32, BF16, I32 = jnp.float32, jnp.bfloat16, jnp.int32


def grid_of(owners):
    side = 8 if owners == 128 else 2
    return side, side


def iota(shape, axis):
    return lax.broadcasted_iota(I32, shape, axis)


def kernel(
    cfg,
    hidden_ref, gain_ref, w1_ref, w2_ref, codes_ref, book_ref, embed_ref, size_ref,
    resid_out, cluster_out, avg_out, new_out,
    hid, book, embed, w1, w2, outv, avgv, newv, cluster,
    flat8, book8, r8, tot8, onehot, idxexp,
    table, items, slots, zgot, ysrc, ygot, want, picked, xcount,
    items_s, slots_s, want_s,
    qsend0, qsend1, qsend2, qrecv0, qrecv1, qrecv2,
    rsend0, rsend1, rsend2, rrecv0, rrecv1, rrecv2,
    xsum0, xsum1, xsum2,
    lsem, ssem, zsend, zrecv, ysend, yrecv, wsend, wrecv, fsend, frecv,
    qss, qrs, rss, rrs, xss, xrs, css, crs, osem,
):
    ny, nz, nx, rows, levels, code_dev = cfg
    owners = ny * nz * CORES
    nyc = ny * CORES
    width = nz * 16
    qsend, qrecv = (qsend0, qsend1, qsend2), (qrecv0, qrecv1, qrecv2)
    rsend, rrecv = (rsend0, rsend1, rsend2), (rrecv0, rrecv1, rrecv2)
    xsum = (xsum0, xsum1, xsum2)
    me = lax.axis_index("code")
    xi = lax.axis_index("item")
    core = lax.rem(me, CORES)
    z = lax.rem(lax.div(me, CORES), nz)
    y = lax.div(me, CORES * nz)
    yc = y * CORES + core
    sibling = me + 1 - 2 * core
    cores = (core, 1 - core)
    columns = [lax.rem(z + a, nz) for a in range(nz)]

    def code_id(ty, tz, tc):
        return (ty * nz + tz) * CORES + tc

    zmates = [(columns[a], code_id(y, columns[a], core)) for a in range(1, nz)]
    ymates = [
        (lax.rem(y + a, ny) * CORES + cores[c], code_id(lax.rem(y + a, ny), z, cores[c]))
        for a in range(ny)
        for c in range(CORES)
        if (a, c) != (0, 0)
    ]

    def sweep(build, send, turn):
        def group(b, first=False):
            partners = []
            for a in range(nz):
                if turn[2]:
                    tz = lax.rem(z + 2 * nz + turn[0] * (a + b), nz)
                    ty = lax.rem(y + ny + turn[1] * a, ny)
                else:
                    tz = columns[turn[0] * a % nz]
                    ty = lax.rem(y + 2 * ny + turn[1] * (a + b), ny)
                for c in range(CORES):
                    if not (first and a == 0 and c == 0):
                        partners.append((code_id(ty, tz, cores[c]), ty * CORES + cores[c], tz))
            for one in partners:
                build(*one)
            for one in partners:
                send(one[0])

        loop(1, ny, group)
        group(0, first=True)

    def loop(low, high, step, unroll=1):
        def go(k, _):
            step(k)
            return 0

        lax.fori_loop(low, high, go, 0, unroll=unroll)

    def wait_bytes(view, sem):
        pltpu.make_async_copy(view, view, sem).wait()

    loads = [
        pltpu.make_async_copy(hidden_ref, hid, lsem.at[0]),
        pltpu.make_async_copy(book_ref, book, lsem.at[1]),
        pltpu.make_async_copy(w1_ref, w1.at[xi], lsem.at[2]),
        pltpu.make_async_copy(w2_ref, w2.at[xi], lsem.at[3]),
        pltpu.make_async_copy(embed_ref, embed, lsem.at[4]),
    ]
    for one in loads:
        one.start()

    barrier = pltpu.get_barrier_semaphore()

    def greet(device):
        pl.semaphore_signal(barrier, inc=1, device_id=device, device_id_type=MESH)

    for _, device in zmates + ymates:
        greet({"code": device})
    for d in range(1, nx):
        greet({"item": lax.rem(xi + d, nx)})

    lane = iota((rows, LANES), 1)
    down, across = iota((rows, rows), 0), iota((rows, rows), 1)
    to_lane = iota((owners, LANES), 1)
    to_sub = iota((owners, rows), 0)
    requests = jnp.zeros((owners, LANES), I32)
    items[...] = jnp.zeros(items.shape, I32)
    slots[...] = jnp.zeros(slots.shape, I32)
    for level in range(levels):
        code_row = codes_ref[level : level + 1, :]
        owner_row = code_row // code_dev
        owner_col = jnp.sum(jnp.where(down == across, owner_row, 0), axis=1, keepdims=True)
        same = owner_col == owner_row
        rank_row = jnp.sum(jnp.where(same & (down < across), 1, 0), axis=0, keepdims=True)
        rank_col = jnp.sum(jnp.where(same & (across < down), 1, 0), axis=1, keepdims=True)
        slots[level : level + 1, :rows] = owner_row
        slots[levels + level : levels + level + 1, :rows] = rank_row
        ring = owner_row // CORES % nz * nyc + owner_row // (CORES * nz) * CORES + owner_row % CORES
        for k in range(2):
            at = 2 * level + k
            chosen = jnp.where((to_sub == ring) & (rank_row == k), code_row % code_dev + 1, 0)
            local = jnp.sum(chosen, axis=1, keepdims=True)
            requests = jnp.where(to_lane == z * 8 + at, local, requests)
            number = jnp.where((lane == owner_col) & (rank_col == k), iota((rows, LANES), 0), 0)
            items[at : at + 1, :] = jnp.sum(number, axis=0, keepdims=True)
    table[...] = requests
    to_smem = [
        pltpu.make_async_copy(items, items_s, ssem.at[0]),
        pltpu.make_async_copy(slots, slots_s, ssem.at[1]),
    ]
    for one in to_smem:
        one.start()

    pl.semaphore_wait(barrier, nz - 1 + nyc - 1 + nx - 1)

    def ring_rows(tz):
        return pl.ds(pl.multiple_of(tz * nyc, nyc), nyc)

    for tz, device in zmates:
        pltpu.make_async_remote_copy(
            src_ref=table.at[ring_rows(tz)], dst_ref=zgot.at[z], send_sem=zsend, recv_sem=zrecv,
            device_id={"code": device}, device_id_type=MESH,
        ).start()

    zgot[z] = table[ring_rows(z), :]

    half = w1.shape[1] // CORES
    weights = (w1, w2)

    def part(w, source, which):
        return w.at[source, pl.ds(pl.multiple_of(which * half, half), half)]

    def weight_copy(i, d):
        return pltpu.make_async_remote_copy(
            src_ref=part(weights[i], xi, core), dst_ref=part(weights[i], xi, core),
            send_sem=wsend.at[i, d - 1], recv_sem=wrecv.at[i, d - 1],
            device_id={"item": lax.rem(xi + d, nx)}, device_id_type=MESH,
        )

    def pass_on(i, d):
        source = lax.rem(xi + nx - d, nx)
        return pltpu.make_async_remote_copy(
            src_ref=part(weights[i], source, core), dst_ref=part(weights[i], source, core),
            send_sem=fsend.at[i, d - 1], recv_sem=frecv.at[i, d - 1],
            device_id={"code": sibling}, device_id_type=MESH,
        )

    for i in range(2):
        loads[2 + i].wait()
        for d in range(1, nx):
            weight_copy(i, d).start()

    loads[1].wait()
    for level in range(levels):
        for c in range(CHUNKS):
            flat8[pl.ds(c, code_dev, stride=CHUNKS), :] = book[level, :, c * LANES : (c + 1) * LANES]
        book8[level] = flat8[: code_dev * CHUNKS, :].reshape(code_dev, CHUNKS, LANES)


    wait_bytes(zgot.at[pl.ds(0, nz - 1)], zrecv)
    gathered = zgot[0]
    for s in range(1, nz):
        gathered = gathered + zgot[s]
    ysrc[:nyc, :] = gathered

    def tile_of(at):
        return pl.ds(pl.multiple_of(lax.div(at, 8) * 8, 8), 8)

    for tyc, device in ymates:
        pltpu.make_async_remote_copy(
            src_ref=ysrc.at[tile_of(tyc)], dst_ref=ygot.at[yc], send_sem=ysend, recv_sem=yrecv,
            device_id={"code": device}, device_id_type=MESH,
        ).start()

    ygot[yc] = ysrc[tile_of(yc), :]
    for one in to_smem:
        one.wait()
    wait_bytes(ygot.at[pl.ds(0, nyc - 1)], yrecv)
    mine = iota((nyc, 8, LANES), 1) == lax.rem(yc, 8)
    want[...] = jnp.sum(jnp.where(mine, ygot[...], 0), axis=1) - 1
    picked[...] = jnp.maximum(want[...], 0)
    ask = pltpu.make_async_copy(picked, want_s, ssem.at[2])
    ask.start()

    code_row = iota((code_dev, LANES), 0)
    code_lane = iota((code_dev, LANES), 1)
    hist = jnp.zeros((code_dev, LANES), F32)
    for s in range(nyc):
        hist = hist + (want[s : s + 1, :] == code_row).astype(F32)
    xcount[xi] = jnp.zeros((8, LANES), F32)
    for level in range(levels):
        column = jnp.sum(
            jnp.where((code_lane % 8) // 2 == level, hist, 0.0), axis=1, keepdims=True
        )
        xcount[xi, level : level + 1, :] = jnp.sum(
            jnp.where(code_row == code_lane, column, 0.0), axis=0, keepdims=True
        )
    count_copies = [
        pltpu.make_async_remote_copy(
            src_ref=xcount.at[xi], dst_ref=xcount.at[xi], send_sem=css.at[d - 1], recv_sem=crs.at[d - 1],
            device_id={"item": lax.rem(xi + d, nx)}, device_id_type=MESH,
        )
        for d in range(1, nx)
    ]
    ask.wait()

    reply_turns = ((1, 1, 0), (-1, -1, 1), (1, -1, 1))
    row_turns = ((1, -1, 0), (-1, 1, 1), (-1, -1, 0))

    def reply(level):
        def block(tyc, tz):
            rows_of = [book8[level, want_s[tyc, tz * 8 + (2 * level + k)]] for k in range(2)]
            return jnp.concatenate(rows_of, axis=0).astype(BF16)

        def build(device, tyc, tz):
            qsend[level][device] = block(tyc, tz)

        def send(device):
            pltpu.make_async_remote_copy(
                src_ref=qsend[level].at[device], dst_ref=qrecv[level].at[me],
                send_sem=qss.at[level], recv_sem=qrs.at[level],
                device_id={"code": device}, device_id_type=MESH,
            ).start()

        qrecv[level][me] = block(yc, z)
        sweep(build, send, reply_turns[level])

    def send_rows(level):
        def block(owner):
            rows_of = [r8[items_s[2 * level + k, owner]] for k in range(2)]
            return jnp.concatenate(rows_of, axis=0).astype(BF16)

        def build(device, tyc, tz):
            rsend[level][device] = block(device)

        def send(device):
            pltpu.make_async_remote_copy(
                src_ref=rsend[level].at[device], dst_ref=rrecv[level].at[yc * nz + z],
                send_sem=rss.at[level], recv_sem=rrs.at[level],
                device_id={"code": device}, device_id_type=MESH,
            ).start()

        rrecv[level][yc * nz + z] = block(me)
        sweep(build, send, row_turns[level])

    def subtract(level):
        wait_bytes(qrecv[level].at[pl.ds(0, owners - 1)], qrs.at[level])

        def one(i):
            second = slots_s[levels + level, i].astype(F32)
            pair = qrecv[level][slots_s[level, i]].astype(F32)
            r8[i] = r8[i] - (pair[:CHUNKS] * (1.0 - second) + pair[CHUNKS:] * second)

        loop(0, rows, one, unroll=8)

    reply(0)
    for one in count_copies:
        one.start()
    for d in range(1, nx):
        weight_copy(0, d).wait_recv()
        pass_on(0, d).start()
    reply(1)
    for d in range(1, nx):
        weight_copy(1, d).wait_recv()
        pass_on(1, d).start()

    loads[0].wait()
    values = hid[...].astype(F32)
    power = jnp.mean(values * values, axis=-1, keepdims=True)
    scaled = values * lax.rsqrt(power + norm_eps)
    gain = gain_ref[...].astype(F32)
    for c in range(CHUNKS):
        span = slice(c * LANES, (c + 1) * LANES)
        hid[:, span] = (scaled[:, span] * gain[c : c + 1, :]).astype(BF16)

    depth = w1.shape[1] * nx
    for d in range(1, nx):
        pass_on(0, d).wait_recv()
    pre = jnp.dot(hid[...], w1[...].reshape(depth, -1), preferred_element_type=F32)
    middle = (pre / (1.0 + jnp.exp(-pre))).astype(BF16)
    for d in range(1, nx):
        pass_on(1, d).wait_recv()
    first = jnp.dot(middle, w2[...].reshape(depth, -1), preferred_element_type=F32)
    for c in range(CHUNKS):
        flat8[pl.ds(c, rows, stride=CHUNKS), :] = first[:, c * LANES : (c + 1) * LANES]
    r8[...] = flat8[: rows * CHUNKS, :].reshape(rows, CHUNKS, LANES)

    def sum_copy(level, d):
        return pltpu.make_async_remote_copy(
            src_ref=xsum[level].at[xi], dst_ref=xsum[level].at[xi],
            send_sem=xss.at[level, d - 1], recv_sem=xrs.at[level, d - 1],
            device_id={"item": lax.rem(xi + d, nx)}, device_id_type=MESH,
        )

    def add_up(level):
        spread_from = iota((LANES, width), 0)
        spread_to = iota((LANES, width), 1)
        spread = (spread_from == (spread_to // 16) * 8 + 2 * level + (spread_to % 16) // 8).astype(BF16)
        asked = jnp.dot(want[...].astype(F32).astype(BF16), spread, preferred_element_type=F32)
        idxexp[...] = asked.astype(I32) * CHUNKS + iota((nyc, width), 1) % CHUNKS
        sum_rows = iota((code_dev * CHUNKS, width), 0)
        for s in range(nyc):
            onehot[:, s * width : (s + 1) * width] = (sum_rows == idxexp[s : s + 1, :]).astype(F32).astype(BF16)
        wait_bytes(rrecv[level].at[pl.ds(0, owners - 1)], rrs.at[level])
        got = rrecv[level][...].reshape(owners * 16, LANES)
        sums = jnp.dot(onehot[...], got, preferred_element_type=F32)
        xsum[level][xi] = sums.astype(BF16)
        for d in range(1, nx):
            sum_copy(level, d).start()

    def out_copies(level):
        return (
            pltpu.make_async_copy(avgv.at[level], avg_out.at[level], osem.at[level]),
            pltpu.make_async_copy(newv.at[level], new_out.at[level], osem.at[levels + level]),
        )

    def update(level):
        for d in range(1, nx):
            sum_copy(level, d).wait_recv()
        total = xsum[level][0].astype(F32)
        for x in range(1, nx):
            total = total + xsum[level][x].astype(F32)
        tot8[...] = total
        row = cluster[level : level + 1, :]
        same = iota((code_dev, code_dev), 0) == iota((code_dev, code_dev), 1)
        column = jnp.sum(jnp.where(same, row, 0.0), axis=1, keepdims=True)
        for c in range(CHUNKS):
            span = slice(c * LANES, (c + 1) * LANES)
            part_sum = tot8[pl.ds(c, code_dev, stride=CHUNKS), :]
            average = ema_decay * embed[level, :, span] + (1.0 - ema_decay) * part_sum
            avgv[level, :, span] = average
            newv[level, :, span] = average / column
        for one in out_copies(level):
            one.start()

    loads[4].wait()
    send_rows(0)
    subtract(0)
    send_rows(1)
    subtract(1)
    send_rows(2)
    for one in count_copies:
        one.wait_recv()
    counts = xcount[0]
    for x in range(1, nx):
        counts = counts + xcount[x]
    cluster[...] = ema_decay * size_ref[...] + (1.0 - ema_decay) * counts[:levels, :code_dev]
    cluster_copy = pltpu.make_async_copy(cluster, cluster_out, lsem.at[0])
    cluster_copy.start()
    add_up(0)
    reply(2)
    add_up(1)
    update(0)
    add_up(2)
    update(1)
    update(2)
    subtract(2)
    flat8[: rows * CHUNKS, :] = r8[...].reshape(rows * CHUNKS, LANES)
    for c in range(CHUNKS):
        outv[:, c * LANES : (c + 1) * LANES] = flat8[pl.ds(c, rows, stride=CHUNKS), :].astype(BF16)
    last = pltpu.make_async_copy(outv, resid_out, osem.at[2 * levels])
    last.start()

    wait_bytes(zgot.at[pl.ds(0, nz - 1)], zsend)
    wait_bytes(ygot.at[pl.ds(0, nyc - 1)], ysend)
    for d in range(1, nx):
        for i in range(2):
            weight_copy(i, d).wait_send()
            pass_on(i, d).wait_send()
        count_copies[d - 1].wait_send()
        for level in range(levels):
            sum_copy(level, d).wait_send()
    for level in range(levels):
        wait_bytes(qrecv[level].at[pl.ds(0, owners - 1)], qss.at[level])
        wait_bytes(rrecv[level].at[pl.ds(0, owners - 1)], rss.at[level])
        for one in out_copies(level):
            one.wait()
    last.wait()
    cluster_copy.wait()


def settle(levels, *refs):
    sources, targets, held, came, went = refs[:4], refs[4:8], refs[8:12], refs[12], refs[13]
    views = [(sources[i], held[i], targets[i]) for i in (0, 1)]
    for level in range(levels):
        views += [(sources[i].at[level], held[i].at[level], targets[i].at[level]) for i in (2, 3)]
    loads = [pltpu.make_async_copy(a, b, came.at[i]) for i, (a, b, _) in enumerate(views)]
    stores = [pltpu.make_async_copy(b, c, went.at[i]) for i, (_, b, c) in enumerate(views)]
    for one in loads:
        one.start()
    for load, store in zip(loads, stores):
        load.wait()
        store.start()
    for one in stores:
        one.wait()


def body(hidden, norm_gain, first_weight, second_weight, codes, codebook, embed_avg, cluster_size):
    rows, width = hidden.shape
    owners = lax.axis_size("code")
    nx = lax.axis_size("item")
    levels, code_dev, _ = codebook.shape
    ny, nz = grid_of(owners)
    nyc = ny * CORES
    cfg = (ny, nz, nx, rows, levels, code_dev)
    vmem, dma = pltpu.VMEM, pltpu.SemaphoreType.DMA
    blocks = [vmem((owners, 16, LANES), BF16)] * 12
    anywhere = pl.BlockSpec(memory_space=pl.ANY)
    inside = pl.BlockSpec(memory_space=pltpu.VMEM)
    shapes = (
        jax.ShapeDtypeStruct((rows, width), BF16),
        jax.ShapeDtypeStruct((levels, code_dev), F32),
        jax.ShapeDtypeStruct((levels, code_dev, width), F32),
        jax.ShapeDtypeStruct((levels, code_dev, width), F32),
    )
    results = pl.pallas_call(
        functools.partial(kernel, cfg),
        out_shape=shapes,
        in_specs=[anywhere, inside, anywhere, anywhere, inside, anywhere, anywhere, inside],
        out_specs=(anywhere, anywhere, anywhere, anywhere),
        scratch_shapes=[
            vmem((rows, width), BF16),
            vmem((levels, code_dev, width), F32),
            vmem((levels, code_dev, width), F32),
            vmem((nx,) + first_weight.shape, BF16),
            vmem((nx,) + second_weight.shape, BF16),
            vmem((rows, width), BF16),
            vmem((levels, code_dev, width), F32),
            vmem((levels, code_dev, width), F32),
            vmem((levels, code_dev), F32),
            vmem((max(rows, code_dev) * CHUNKS, LANES), F32),
            vmem((levels, code_dev, CHUNKS, LANES), F32),
            vmem((rows, CHUNKS, LANES), F32),
            vmem((code_dev * CHUNKS, LANES), F32),
            vmem((code_dev * CHUNKS, owners * 16), BF16),
            vmem((nyc, nz * 16), I32),
            vmem((owners, LANES), I32),
            vmem((8, LANES), I32),
            vmem((8, LANES), I32),
            vmem((nz, nyc, LANES), I32),
            vmem((max(nyc, 8), LANES), I32),
            vmem((nyc, 8, LANES), I32),
            vmem((nyc, LANES), I32),
            vmem((nyc, LANES), I32),
            vmem((nx, 8, LANES), F32),
            pltpu.SMEM((8, LANES), I32),
            pltpu.SMEM((8, LANES), I32),
            pltpu.SMEM((nyc, LANES), I32),
            *blocks,
            *[vmem((nx, code_dev * CHUNKS, LANES), BF16)] * 3,
            dma((5,)),
            dma((3,)),
            dma,
            dma,
            dma,
            dma,
            dma((2, nx - 1)),
            dma((2, nx - 1)),
            dma((2, nx - 1)),
            dma((2, nx - 1)),
            dma((levels,)),
            dma((levels,)),
            dma((levels,)),
            dma((levels,)),
            dma((levels, nx - 1)),
            dma((levels, nx - 1)),
            dma((nx - 1,)),
            dma((nx - 1,)),
            dma((2 * levels + 1,)),
        ],
        compiler_params=pltpu.CompilerParams(
            collective_id=0, has_side_effects=True, vmem_limit_bytes=64 << 20
        ),
    )(
        hidden, norm_gain.reshape(CHUNKS, LANES), first_weight, second_weight, codes.T,
        codebook, embed_avg, cluster_size,
    )
    return pl.pallas_call(
        functools.partial(settle, levels),
        out_shape=shapes,
        in_specs=[anywhere] * 4,
        out_specs=(anywhere,) * 4,
        scratch_shapes=[vmem(x.shape, x.dtype) for x in shapes] + [dma((2 + 2 * levels,))] * 2,
        compiler_params=pltpu.CompilerParams(vmem_limit_bytes=64 << 20),
    )(*results)


def solution(mesh):
    in_specs = (
        P(("code", "item"), None),
        P(),
        P("item", None),
        P("item", None),
        P(("code", "item"), None),
        P(None, "code", None),
        P(None, "code", None),
        P(None, "code"),
    )
    out_specs = (
        P(("code", "item"), None),
        P(None, "code"),
        P(None, "code", None),
        P(None, "code", None),
    )
    return jax.shard_map(body, mesh=mesh, in_specs=in_specs, out_specs=out_specs, check_vma=False)
```
